128 devices in a mesh: ctx: 8 (over y_lo, z), tp: 16 (over x, y_hi, core).
Axes of the slice: x: 4, y: 4 (y_hi: 2, y_lo: 2; y = y_hi * 2 + y_lo), z: 4, core: 2. Of those that a mesh axis runs over, the one named last changes fastest.
Arguments:
- key_feature: bfloat16 [4096, 16384], P('tp', 'ctx'), may hold values from -6 to 6
- value_feature: bfloat16 [4096, 16384], P('tp', 'ctx'), may hold values from -6 to 6
- query_gate: bfloat16 [4096, 16384], P('tp', 'ctx'), may hold values from -6 to 6
- decay_rates: float32 [16, 4096], P(None, 'tp'), may hold values from 1.8310547e-05 to 0.05
- residues: float32 [16, 4096], P(None, 'tp'), may hold values from -4 to 4
- skip_gain: float32 [4096], P('tp'), may hold values from -1 to 1
- out_weight: bfloat16 [4096, 4096], P('tp'), may hold values from -0.125 to 0.125
Outputs:
- mixed_out: bfloat16 [4096, 16384], P('tp', 'ctx')
The draws below stay inside these ranges and needn't reach their ends.
All inputs are finite; a program needn't handle non-finite values.
Results may differ from the reference program's by a relative error of at most 0.02.
Values may be sent and summed in bfloat16 or wider, within the bound.
A program may use at most 128 MiB of HBM per device.

```python
import math
import jax
import jax.numpy as jnp
from jax import lax

D = 4096
MODES = 16
LEN = 16384


def draw_decay_rates(key, part):
    key = jax.random.fold_in(key, 7)
    slow_key = jax.random.fold_in(key, 0)
    return jnp.exp(jax.random.uniform(slow_key, (MODES, D), jnp.float32, math.log(0.5 / LEN), math.log(0.05)))


def with_spikes(drawn, stream_key, source, target, blocks, factor):
    def block_of(axis_at):
        return (jnp.arange(drawn.shape[axis_at]) // (drawn.shape[axis_at] // blocks)).reshape((-1,) + (1,) * (drawn.ndim - 1 - axis_at))

    near = jax.random.permutation(stream_key, blocks)[block_of(target)]
    far = (block_of(target) + blocks // 2) % blocks
    return jnp.where((block_of(source) == near) | (block_of(source) == far), factor * drawn, drawn)


def levels(key, shape, cuts, least, largest):
    gain = 1.0
    for dim, shards_of in cuts:
        steps = jax.random.uniform(jax.random.fold_in(jax.random.fold_in(key, 6), dim), (shards_of,), jnp.float32, least / len(cuts), largest / len(cuts))
        gain = gain * jnp.repeat(jnp.exp(steps), shape[dim] // shards_of).reshape((-1,) + (1,) * (len(shape) - 1 - dim))
    return gain


def scatter_about(own_key, extent, width, bound, pieces=(), held_as=jnp.bfloat16):
    level = levels(own_key, extent, pieces, -0.22, 0.18) if pieces else 1.0
    array = jax.random.normal(own_key, extent, jnp.float32) * width * level
    return jnp.minimum(jnp.maximum(array, -bound), bound).astype(held_as)


def bell_draw_with(stream_key, shape, scale, most, pieces, heavy, held_as=jnp.bfloat16):
    values = scale * jax.random.normal(stream_key, shape, jnp.float32)
    if pieces:
        values = values * levels(stream_key, shape, pieces, -0.22, 0.18)
    return jnp.clip(with_spikes(values, jax.random.fold_in(stream_key, 3), *heavy), -most, most).astype(held_as)


def setup_inputs(seed: int = 0) -> dict:
    streams_of = jax.random.split(jax.random.key(seed), 8)
    key_feature = scatter_about(streams_of[0], (D, LEN), 1.0, 6.0, ((0, 16), (1, 8)))
    value_feature = scatter_about(streams_of[1], (D, LEN), 1.0, 6.0, ((0, 16), (1, 8)))
    query_gate = scatter_about(streams_of[2], (D, LEN), 1.0, 6.0, ((0, 16), (1, 8)))
    decay_rates = draw_decay_rates(jax.random.fold_in(streams_of[7], 71), 0)
    residues = scatter_about(streams_of[4], (MODES, D), 1.0, 4.0, ((1, 16),), jnp.float32)
    skip_gain = jnp.clip(jax.random.uniform(streams_of[5], (D,), jnp.float32, -1.0, 1.0) * levels(streams_of[5], (D,), ((0, 16),), -0.4, 0.0), -1.0, 1.0)
    out_weight = bell_draw_with(streams_of[6], (D, D), D ** -0.5, 0.125, ((0, 16),), (0, 1, 16, 2.0))
    return dict(key_feature=key_feature, value_feature=value_feature, query_gate=query_gate, decay_rates=decay_rates, residues=residues, skip_gain=skip_gain, out_weight=out_weight)


def filter_taps(rates, weights, offsets):
    taps = jnp.zeros((rates.shape[1], offsets.shape[0]), jnp.float32)
    for harmonic in range(rates.shape[0]):
        scale_row = weights[harmonic] * jnp.sqrt(2.0 * rates[harmonic] / rates.shape[0])
        taps = taps + scale_row[:, None] * jnp.exp(-rates[harmonic][:, None] * offsets[None, :])
    return taps

def reference(key_feature, value_feature, query_gate, decay_rates, residues, skip_gain, out_weight):
    product = (key_feature.astype(jnp.float32) * value_feature.astype(jnp.float32)).astype(jnp.bfloat16)
    offsets = jnp.arange(LEN).astype(jnp.float32)
    groups = 16
    width_block = D // groups

    def one_block(block_index):
        start_row = block_index * width_block
        signal = lax.dynamic_slice_in_dim(product, start_row, width_block, 0).astype(jnp.float32)
        rates = lax.dynamic_slice_in_dim(decay_rates, start_row, width_block, 1)
        weights = lax.dynamic_slice_in_dim(residues, start_row, width_block, 1)
        gains = lax.dynamic_slice_in_dim(skip_gain, start_row, width_block, 0)
        taps = filter_taps(rates, weights, offsets)
        spectra = jnp.fft.rfft(signal, n=2 * LEN) * jnp.fft.rfft(taps, n=2 * LEN)
        causal = jnp.fft.irfft(spectra, n=2 * LEN)[:, :LEN]
        return causal + gains[:, None] * signal
    filtered = lax.map(one_block, jnp.arange(groups, dtype=jnp.int32)).reshape(D, LEN)
    gated = (query_gate.astype(jnp.float32) * filtered).astype(jnp.bfloat16)
    return jnp.dot(out_weight.T, gated, preferred_element_type=jnp.float32).astype(jnp.bfloat16)
```

```python
import functools

import jax
import jax.numpy as jnp
from jax import lax
from jax.experimental import pallas as pl
from jax.experimental.pallas import tpu as pltpu
from jax.sharding import PartitionSpec as P

MESH = pl.DeviceIdType.MESH

MODES = 16
CH = 256
TOK = 2048
CHUNK = 256
NC = TOK // CHUNK
SUB = 32
LANES = 128
CTX = 8
NX = 4
SLOTS = 8

XP, XM, CO, F0, F1, CXM, CXP, C0, C1, YY = range(10)
LAG_FWD, LAG_OPP, LAG_MM, LAG_FIN = 1, 2, 3, 5


def kernel(
    key_hbm, val_hbm, gate_hbm, rate_ref, res_ref, skip_ref, w_hbm, out_hbm,
    keyb, valb, gateb, xt, est, gtot, am1, am2, am4, apow, coef, carry, fr,
    g, w, wt, pself, ysend, yrecv, ostage,
    in_sem, out_sem, ss, rs, fss, frs, wss, wrs,
):
    ctx = lax.axis_index("ctx")
    tp = lax.axis_index("tp")
    x = tp // 4
    yh = (tp // 2) % 2
    core = tp % 2

    def dev(dx, dy, dc):
        return (ctx, ((x + dx) % NX) * 4 + ((yh + dy) % 2) * 2 + (core + dc) % 2)

    def peer(d):
        return ((ctx + d) % CTX, tp)

    x_next, x_prev, other, y_dev = dev(1, 0, 0), dev(3, 0, 0), dev(0, 0, 1), dev(0, 1, 0)
    plane = [(dx, dc) for dx in range(NX) for dc in range(2) if (dx, dc) != (0, 0)]

    barrier = pltpu.get_barrier_semaphore()
    for dx, dc in plane:
        pl.semaphore_signal(barrier, inc=1, device_id=dev(dx, 0, dc), device_id_type=MESH)
    pl.semaphore_signal(barrier, inc=1, device_id=y_dev, device_id_type=MESH)
    for d in range(1, CTX):
        pl.semaphore_signal(barrier, inc=1, device_id=peer(d), device_id_type=MESH)

    loads = [
        pltpu.make_async_copy(key_hbm, keyb, in_sem.at[0]),
        pltpu.make_async_copy(val_hbm, valb, in_sem.at[1]),
        pltpu.make_async_copy(gate_hbm, gateb, in_sem.at[2]),
    ]
    for c in loads:
        c.start()

    def slot_of(dx, dc):
        return ((x + dx) % NX) * 2 + (core + dc) % 2

    me_slot = slot_of(0, 0)

    def w_cols(dx, dc, yb):
        col = (((x + dx) % NX) * 4 + yb * 2 + (core + dc) % 2) * CH
        return w_hbm.at[:, pl.ds(pl.multiple_of(col, CH), CH)]

    own_w = [
        pltpu.make_async_copy(w_cols(0, 0, yb), w.at[me_slot, yb], in_sem.at[3 + yb]) for yb in range(2)
    ]
    for c in own_w:
        c.start()

    pl.semaphore_wait(barrier, len(plane) + 1 + CTX - 1)

    def w_copy(dx, dc, yb, slot):
        i = dx * 2 + dc
        return pltpu.make_async_remote_copy(
            w_cols(dx, dc, yb), w.at[slot, yb], wss.at[i, yb], wrs.at[i, yb],
            device_id=dev(dx, 0, dc), device_id_type=MESH,
        )

    for dx, dc in plane:
        for yb in range(2):
            w_copy(dx, dc, yb, me_slot).start()

    rate = rate_ref[...]
    for m in range(MODES):
        r8 = jnp.broadcast_to(rate[m : m + 1, :], (8, CH))
        sub = lax.broadcasted_iota(jnp.int32, (8, CH), 0)
        subf = sub.astype(jnp.float32)
        am1[m] = jnp.where(sub >= 1, jnp.exp(-r8 * float(SUB)), 0.0)
        am2[m] = jnp.where(sub >= 2, jnp.exp(-r8 * float(2 * SUB)), 0.0)
        am4[m] = jnp.where(sub >= 4, jnp.exp(-r8 * float(4 * SUB)), 0.0)
        apow[m] = jnp.exp(-r8 * (subf * float(SUB)))
    coef[0] = jnp.exp(-rate)
    coef[1] = res_ref[...] * jnp.sqrt(2.0 * rate / MODES)
    coef[2] = jnp.exp(-rate * float(CHUNK))

    loads[0].wait()
    loads[1].wait()

    def pass1(n, c0):
        ts = pl.ds(pl.multiple_of(n * CHUNK, CHUNK), CHUNK)
        prod = (keyb[:, ts].astype(jnp.float32) * valb[:, ts].astype(jnp.float32)).astype(jnp.bfloat16)
        prod = prod.astype(jnp.float32).T
        for h in range(CH // LANES):
            xt[h, ts, :] = prod[:, h * LANES : (h + 1) * LANES]
        for h in range(CH // LANES):
            ls = slice(h * LANES, (h + 1) * LANES)
            a = [jnp.broadcast_to(coef[0, m : m + 1, ls], (8, LANES)) for m in range(MODES)]

            def step(i, hs):
                for u in range(4):
                    xv = xt[h, pl.ds(n * CHUNK + i * 4 + u, 8, stride=SUB), :]
                    hs = tuple(a[m] * hs[m] + xv for m in range(MODES))
                return hs

            hs = lax.fori_loop(0, SUB // 4, step, tuple(jnp.zeros((8, LANES), jnp.float32) for _ in range(MODES)))
            first = lax.broadcasted_iota(jnp.int32, (8, LANES), 0) == 0
            for m in range(MODES):
                s = hs[m]
                s = s + am1[m, :, ls] * pltpu.roll(s, 1, 0)
                s = s + am2[m, :, ls] * pltpu.roll(s, 2, 0)
                s = s + am4[m, :, ls] * pltpu.roll(s, 4, 0)
                est[n, m, :, ls] = jnp.where(first, 0.0, pltpu.roll(s, 1, 0))
                gtot[n, m : m + 1, ls] = s[7:8, :]
        return c0

    lax.fori_loop(0, NC, pass1, 0)

    final = jnp.zeros((MODES, CH), jnp.float32)
    for n in range(NC):
        final = coef[2] * final + gtot[n]
    fr[ctx] = final

    def state_copy(d, slot):
        return pltpu.make_async_remote_copy(
            fr.at[slot], fr.at[slot], fss.at[d], frs.at[d], device_id=peer(d), device_id_type=MESH
        )

    for d in range(1, CTX):
        state_copy(d, ctx).start()
    loads[2].wait()
    for d in range(1, CTX):
        state_copy(d, (ctx + CTX - d) % CTX).wait_recv()
    start = jnp.zeros((MODES, CH), jnp.float32)
    for j in range(CTX):
        gap = jnp.maximum(ctx - 1 - j, 0).astype(jnp.float32) * float(TOK)
        start = start + jnp.where(j < ctx, jnp.exp(-rate * gap) * fr[j], 0.0)
    carry[...] = start

    def conv(n):
        for h in range(CH // LANES):
            ls = slice(h * LANES, (h + 1) * LANES)
            a = [jnp.broadcast_to(coef[0, m : m + 1, ls], (8, LANES)) for m in range(MODES)]
            b = [jnp.broadcast_to(coef[1, m : m + 1, ls], (8, LANES)) for m in range(MODES)]
            skip = jnp.broadcast_to(skip_ref[:, ls], (8, LANES))

            def step(i, hs):
                for u in range(4):
                    at = pl.ds(n * CHUNK + i * 4 + u, 8, stride=SUB)
                    xv = xt[h, at, :]
                    hs = tuple(a[m] * hs[m] + xv for m in range(MODES))
                    terms = [skip * xv] + [b[m] * hs[m] for m in range(MODES)]
                    while len(terms) > 1:
                        terms = [
                            terms[q] + terms[q + 1] if q + 1 < len(terms) else terms[q]
                            for q in range(0, len(terms), 2)
                        ]
                    xt[h, at, :] = terms[0]
                return hs

            hs = tuple(
                est[n, m, :, ls] + apow[m, :, ls] * carry[m : m + 1, ls] for m in range(MODES)
            )
            lax.fori_loop(0, SUB // 4, step, hs)
        carry[...] = coef[2] * carry[...] + gtot[n]
        ts = pl.ds(pl.multiple_of(n * CHUNK, CHUNK), CHUNK)
        for h in range(CH // LANES):
            filtered = xt[h, ts, :].T
            rows = pl.ds(pl.multiple_of(me_slot * CH + h * LANES, LANES), LANES)
            gate = gateb[h * LANES : (h + 1) * LANES, ts].astype(jnp.float32)
            g[n, rows, :] = (gate * filtered).astype(jnp.bfloat16)

    def copy(kind, n, slot, device, half=None):
        first = slot * CH + (0 if half is None else half * (CH // 2))
        size = CH if half is None else CH // 2
        ref = g.at[n, pl.ds(pl.multiple_of(first, size), size), :]
        return pltpu.make_async_remote_copy(
            ref, ref, ss.at[kind, n], rs.at[kind, n], device_id=device, device_id_type=MESH
        )

    def y_copy(n):
        return pltpu.make_async_remote_copy(
            ysend.at[n], yrecv.at[n], ss.at[YY, n], rs.at[YY, n], device_id=y_dev, device_id_type=MESH
        )

    def out_copy(n):
        ts = pl.ds(pl.multiple_of(n * CHUNK, CHUNK), CHUNK)
        return pltpu.make_async_copy(ostage.at[n], out_hbm.at[:, ts], out_sem.at[n])

    s_prev, s_next, s_opp = slot_of(3, 0), slot_of(1, 0), slot_of(2, 0)
    o_me, o_prev, o_next, o_opp = slot_of(0, 1), slot_of(3, 1), slot_of(1, 1), slot_of(2, 1)

    def forward(n):
        copy(XP, n, s_prev, x_next).wait_recv()
        copy(F0, n, s_prev, x_next, 0).start()
        copy(CXM, n, s_prev, other).start()
        copy(XM, n, s_next, x_prev).wait_recv()
        copy(F1, n, s_next, x_prev, 1).start()
        copy(CXP, n, s_next, other).start()

    def opposite(n):
        copy(F0, n, s_opp, x_next, 0).wait_recv()
        copy(C0, n, s_opp, other, 0).start()
        copy(F1, n, s_opp, x_prev, 1).wait_recv()
        copy(C1, n, s_opp, other, 1).start()

    def weights():
        for c in own_w:
            c.wait()
        for dx, dc in plane:
            for yb in range(2):
                w_copy(dx, dc, yb, slot_of(NX - dx, dc)).wait_recv()
        for s in range(SLOTS):
            for yb in range(2):
                wt[yb * CH : (yb + 1) * CH, s * CH : (s + 1) * CH] = w[s, yb].T

    def project(n):
        copy(CO, n, o_me, other).wait_recv()
        copy(CXM, n, o_prev, other).wait_recv()
        copy(CXP, n, o_next, other).wait_recv()
        copy(C0, n, o_opp, other, 0).wait_recv()
        copy(C1, n, o_opp, other, 1).wait_recv()
        theirs = pl.ds(pl.multiple_of((1 - yh) * CH, CH), CH)
        mine = pl.ds(pl.multiple_of(yh * CH, CH), CH)
        ysend[n] = jnp.dot(wt[theirs, :], g[n], preferred_element_type=jnp.float32).astype(jnp.bfloat16)
        y_copy(n).start()
        pself[n] = jnp.dot(wt[mine, :], g[n], preferred_element_type=jnp.float32)

    def finish(n):
        y_copy(n).wait_recv()
        ostage[n] = (pself[n] + yrecv[n].astype(jnp.float32)).astype(jnp.bfloat16)
        out_copy(n).start()

    def turn(i, c0):
        @pl.when(i < NC)
        def _():
            conv(i)
            copy(XP, i, me_slot, x_next).start()
            copy(XM, i, me_slot, x_prev).start()
            copy(CO, i, me_slot, other).start()

        def at(lag, f):
            @pl.when(jnp.logical_and(i >= lag, i < NC + lag))
            def _():
                f(i - lag)

        at(LAG_FWD, forward)
        at(LAG_OPP, opposite)

        @pl.when(i == LAG_MM)
        def _():
            weights()

        at(LAG_MM, project)
        at(LAG_FIN, finish)
        return c0

    lax.fori_loop(0, NC + LAG_FIN, turn, 0)

    def drain(n, c0):
        copy(XP, n, me_slot, x_next).wait_send()
        copy(XM, n, me_slot, x_prev).wait_send()
        copy(CO, n, me_slot, other).wait_send()
        copy(F0, n, s_prev, x_next, 0).wait_send()
        copy(F1, n, s_next, x_prev, 1).wait_send()
        copy(CXM, n, s_prev, other).wait_send()
        copy(CXP, n, s_next, other).wait_send()
        copy(C0, n, s_opp, other, 0).wait_send()
        copy(C1, n, s_opp, other, 1).wait_send()
        y_copy(n).wait_send()
        out_copy(n).wait()
        return c0

    lax.fori_loop(0, NC, drain, 0)
    for dx, dc in plane:
        for yb in range(2):
            w_copy(dx, dc, yb, me_slot).wait_send()
    for d in range(1, CTX):
        state_copy(d, ctx).wait_send()


def on_device(key_feature, value_feature, query_gate, decay_rates, residues, skip_gain, out_weight):
    anywhere = pl.BlockSpec(memory_space=pl.ANY)
    local = pl.BlockSpec(memory_space=pltpu.VMEM)
    bf16, f32 = jnp.bfloat16, jnp.float32
    return pl.pallas_call(
        kernel,
        out_shape=jax.ShapeDtypeStruct((CH, TOK), bf16),
        in_specs=[anywhere, anywhere, anywhere, local, local, local, anywhere],
        out_specs=anywhere,
        scratch_shapes=[
            pltpu.VMEM((CH, TOK), bf16),
            pltpu.VMEM((CH, TOK), bf16),
            pltpu.VMEM((CH, TOK), bf16),
            pltpu.VMEM((CH // LANES, TOK, LANES), f32),
            pltpu.VMEM((NC, MODES, 8, CH), f32),
            pltpu.VMEM((NC, MODES, CH), f32),
            pltpu.VMEM((MODES, 8, CH), f32),
            pltpu.VMEM((MODES, 8, CH), f32),
            pltpu.VMEM((MODES, 8, CH), f32),
            pltpu.VMEM((MODES, 8, CH), f32),
            pltpu.VMEM((3, MODES, CH), f32),
            pltpu.VMEM((MODES, CH), f32),
            pltpu.VMEM((CTX, MODES, CH), f32),
            pltpu.VMEM((NC, SLOTS * CH, CHUNK), bf16),
            pltpu.VMEM((SLOTS, 2, CH, CH), bf16),
            pltpu.VMEM((2 * CH, SLOTS * CH), bf16),
            pltpu.VMEM((NC, CH, CHUNK), f32),
            pltpu.VMEM((NC, CH, CHUNK), bf16),
            pltpu.VMEM((NC, CH, CHUNK), bf16),
            pltpu.VMEM((NC, CH, CHUNK), bf16),
            pltpu.SemaphoreType.DMA((5,)),
            pltpu.SemaphoreType.DMA((NC,)),
            pltpu.SemaphoreType.DMA((10, NC)),
            pltpu.SemaphoreType.DMA((10, NC)),
            pltpu.SemaphoreType.DMA((CTX,)),
            pltpu.SemaphoreType.DMA((CTX,)),
            pltpu.SemaphoreType.DMA((SLOTS, 2)),
            pltpu.SemaphoreType.DMA((SLOTS, 2)),
        ],
        compiler_params=pltpu.CompilerParams(
            collective_id=0, has_side_effects=True, vmem_limit_bytes=56 * 2**20
        ),
        name="hyena",
    )(
        key_feature, value_feature, query_gate, decay_rates, residues,
        skip_gain.reshape(1, CH), out_weight,
    )


def solution(mesh):
    return jax.shard_map(
        on_device,
        mesh=mesh,
        in_specs=(
            P("tp", "ctx"), P("tp", "ctx"), P("tp", "ctx"),
            P(None, "tp"), P(None, "tp"), P("tp"), P("tp", None),
        ),
        out_specs=P("tp", "ctx"),
        check_vma=False,
    )
```

```python
import functools

import jax
import jax.numpy as jnp
from jax import lax
from jax.experimental import pallas as pl
from jax.experimental.pallas import tpu as pltpu
from jax.sharding import PartitionSpec as P

MESH = pl.DeviceIdType.MESH

MODES = 16
CH = 256
TOK = 2048
CHUNK = 256
NC = TOK // CHUNK
NU = NC + 1
SUB = 32
PITCH = 40
LANES = 128
CTX = 8
NX = 4
SLOTS = 8
W_DIRECT = 64
W_PART = (CH - W_DIRECT) // 4

XP, XM, CO, F0, F1, CXM, CXP, C0, C1, YY = range(10)
LAG_FWD, LAG_OPP, LAG_MM, LAG_FIN = 1, 2, 4, 6


def kernel(
    key_hbm, val_hbm, gate_hbm, rate_ref, res_ref, skip_ref, w_hbm, out_ref,
    keyb, valb, gateb, xt, est, gtot, am1, am2, am4, apow, coef, carry, fr,
    g, w, pself, ysend, yrecv,
    in_sem, ss, rs, fss, frs, wss, wrs, zss, zrs,
):
    ctx = lax.axis_index("ctx")
    tp = lax.axis_index("tp")
    x = tp // 4
    yh = (tp // 2) % 2
    core = tp % 2

    def dev(dx, dy, dc):
        return (ctx, ((x + dx) % NX) * 4 + ((yh + dy) % 2) * 2 + (core + dc) % 2)

    def peer(d):
        return ((ctx + d) % CTX, tp)

    x_next, x_prev, other, y_dev = dev(1, 0, 0), dev(3, 0, 0), dev(0, 0, 1), dev(0, 1, 0)
    plane = [(dx, dc) for dx in range(NX) for dc in range(2) if (dx, dc) != (0, 0)]

    barrier = pltpu.get_barrier_semaphore()
    for dx, dc in plane:
        pl.semaphore_signal(barrier, inc=1, device_id=dev(dx, 0, dc), device_id_type=MESH)
    pl.semaphore_signal(barrier, inc=1, device_id=y_dev, device_id_type=MESH)
    for d in range(1, CTX):
        pl.semaphore_signal(barrier, inc=1, device_id=peer(d), device_id_type=MESH)

    loads = [
        pltpu.make_async_copy(key_hbm, keyb, in_sem.at[0]),
        pltpu.make_async_copy(val_hbm, valb, in_sem.at[1]),
        pltpu.make_async_copy(gate_hbm, gateb, in_sem.at[2]),
    ]
    for c in loads:
        c.start()

    def slot_of(dx, dc):
        return ((x + dx) % NX) * 2 + (core + dc) % 2

    me_slot = slot_of(0, 0)

    z = ctx % 4

    def z_rows(d):
        return pl.ds(pl.multiple_of(W_DIRECT + ((z + d) % 4) * W_PART, 16), W_PART)

    w_rows = (z_rows(0), pl.ds(0, W_DIRECT))

    def w_cols(dx, dc, yb, part):
        col = (((x + dx) % NX) * 4 + yb * 2 + (core + dc) % 2) * CH
        return w_hbm.at[w_rows[part], pl.ds(pl.multiple_of(col, CH), CH)]

    own_w = [
        pltpu.make_async_copy(
            w_cols(0, 0, yb, part), w.at[me_slot, yb, w_rows[part]], in_sem.at[3 + part * 2 + yb]
        )
        for part in range(2)
        for yb in range(2)
    ]
    for c in own_w:
        c.start()

    def w_copy(dx, dc, yb, part, slot):
        i = dx * 2 + dc
        return pltpu.make_async_remote_copy(
            w_cols(dx, dc, yb, part), w.at[slot, yb, w_rows[part]], wss.at[i, yb, part], wrs.at[i, yb, part],
            device_id=dev(dx, 0, dc), device_id_type=MESH,
        )

    def z_copy(d, rows):
        part = w.at[:, :, rows, :]
        return pltpu.make_async_remote_copy(
            part, part, zss.at[d], zrs.at[d],
            device_id=((ctx // 4) * 4 + (z + d) % 4, tp), device_id_type=MESH,
        )

    rate = rate_ref[...]
    for m in range(MODES):
        r8 = jnp.broadcast_to(rate[m : m + 1, :], (8, CH))
        sub = lax.broadcasted_iota(jnp.int32, (8, CH), 0)
        subf = sub.astype(jnp.float32)
        am1[m] = jnp.where(sub >= 1, jnp.exp(-r8 * float(SUB)), 0.0)
        am2[m] = jnp.where(sub >= 2, jnp.exp(-r8 * float(2 * SUB)), 0.0)
        am4[m] = jnp.where(sub >= 4, jnp.exp(-r8 * float(4 * SUB)), 0.0)
        apow[m] = jnp.exp(-r8 * (subf * float(SUB)))
    coef[0] = jnp.exp(-rate)
    coef[1] = res_ref[...] * jnp.sqrt(2.0 * rate / MODES)
    coef[2] = jnp.exp(-rate * float(CHUNK))

    pl.semaphore_wait(barrier, len(plane) + 1 + CTX - 1)
    for part in range(2):
        for dx, dc in plane:
            for yb in range(2):
                w_copy(dx, dc, yb, part, me_slot).start()

    loads[0].wait()
    loads[1].wait()

    def sub_rows(n, q):
        return pl.ds(pl.multiple_of((n * 8 + q) * PITCH, 8), SUB)

    def step_rows(n, i):
        return pl.ds(n * (8 * PITCH) + i, 8, stride=PITCH)

    def pass1(n, c0):
        ts = pl.ds(pl.multiple_of(n * CHUNK, CHUNK), CHUNK)
        prod = (keyb[:, ts].astype(jnp.float32) * valb[:, ts].astype(jnp.float32)).astype(jnp.bfloat16)
        prod = prod.astype(jnp.float32).T
        for h in range(CH // LANES):
            for q in range(8):
                xt[h, sub_rows(n, q), :] = prod[q * SUB : (q + 1) * SUB, h * LANES : (h + 1) * LANES]
        for h in range(CH // LANES):
            ls = slice(h * LANES, (h + 1) * LANES)
            a = [jnp.broadcast_to(coef[0, m : m + 1, ls], (8, LANES)) for m in range(MODES)]

            hs = [jnp.zeros((8, LANES), jnp.float32)] * MODES
            for i in range(SUB):
                xv = xt[h, step_rows(n, i), :]
                hs = [a[m] * hs[m] + xv for m in range(MODES)]
            first = lax.broadcasted_iota(jnp.int32, (8, LANES), 0) == 0
            for m in range(MODES):
                s = hs[m]
                s = s + am1[m, :, ls] * pltpu.roll(s, 1, 0)
                s = s + am2[m, :, ls] * pltpu.roll(s, 2, 0)
                s = s + am4[m, :, ls] * pltpu.roll(s, 4, 0)
                est[n, m, :, ls] = jnp.where(first, 0.0, pltpu.roll(s, 1, 0))
                gtot[n, m : m + 1, ls] = s[7:8, :]
        return c0

    lax.fori_loop(0, NC, pass1, 0)

    final = jnp.zeros((MODES, CH), jnp.float32)
    for n in range(NC):
        final = coef[2] * final + gtot[n]
    fr[ctx] = final

    def state_copy(d, slot):
        return pltpu.make_async_remote_copy(
            fr.at[slot], fr.at[slot], fss.at[d], frs.at[d], device_id=peer(d), device_id_type=MESH
        )

    for d in range(1, CTX):
        state_copy(d, ctx).start()
    loads[2].wait()

    for c in own_w[:2]:
        c.wait()
    for dx, dc in plane:
        for yb in range(2):
            w_copy(dx, dc, yb, 0, slot_of(NX - dx, dc)).wait_recv()
    for d in range(1, 4):
        z_copy(d, z_rows(0)).start()

    for d in range(1, CTX):
        state_copy(d, (ctx + CTX - d) % CTX).wait_recv()
    start = jnp.zeros((MODES, CH), jnp.float32)
    for j in range(CTX):
        gap = jnp.maximum(ctx - 1 - j, 0).astype(jnp.float32) * float(TOK)
        start = start + jnp.where(j < ctx, jnp.exp(-rate * gap) * fr[j], 0.0)
    carry[...] = start

    def conv(n):
        for h in range(CH // LANES):
            ls = slice(h * LANES, (h + 1) * LANES)
            a = [jnp.broadcast_to(coef[0, m : m + 1, ls], (8, LANES)) for m in range(MODES)]
            b = [jnp.broadcast_to(coef[1, m : m + 1, ls], (8, LANES)) for m in range(MODES)]
            skip = jnp.broadcast_to(skip_ref[:, ls], (8, LANES))

            hs = [est[n, m, :, ls] + apow[m, :, ls] * carry[m : m + 1, ls] for m in range(MODES)]
            for i in range(SUB):
                at = step_rows(n, i)
                xv = xt[h, at, :]
                hs = [a[m] * hs[m] + xv for m in range(MODES)]
                terms = [skip * xv] + [b[m] * hs[m] for m in range(MODES)]
                while len(terms) > 1:
                    terms = [
                        terms[q] + terms[q + 1] if q + 1 < len(terms) else terms[q]
                        for q in range(0, len(terms), 2)
                    ]
                xt[h, at, :] = terms[0]
        carry[...] = coef[2] * carry[...] + gtot[n]
        ts = pl.ds(pl.multiple_of(n * CHUNK, CHUNK), CHUNK)
        for h in range(CH // LANES):
            filtered = jnp.concatenate([xt[h, sub_rows(n, q), :] for q in range(8)], axis=0).T
            rows = pl.ds(pl.multiple_of(me_slot * CH + h * LANES, LANES), LANES)
            gate = gateb[h * LANES : (h + 1) * LANES, ts].astype(jnp.float32)
            g[n, rows, :] = (gate * filtered).astype(jnp.bfloat16)

    def lanes_of(u, full):
        if full:
            return u, pl.ds(0, CHUNK)
        return NC - 1, pl.ds(pl.multiple_of((u - (NC - 1)) * LANES, LANES), LANES)

    def copy(kind, u, full, slot, device, half=None):
        n, lanes = lanes_of(u, full)
        first = slot * CH + (0 if half is None else half * (CH // 2))
        size = CH if half is None else CH // 2
        ref = g.at[n, pl.ds(pl.multiple_of(first, size), size), lanes]
        return pltpu.make_async_remote_copy(
            ref, ref, ss.at[kind, u], rs.at[kind, u], device_id=device, device_id_type=MESH
        )

    def y_copy(u, full):
        n, lanes = lanes_of(u, full)
        return pltpu.make_async_remote_copy(
            ysend.at[n, :, lanes], yrecv.at[n, :, lanes], ss.at[YY, u], rs.at[YY, u],
            device_id=y_dev, device_id_type=MESH,
        )

    s_prev, s_next, s_opp = slot_of(3, 0), slot_of(1, 0), slot_of(2, 0)
    o_me, o_prev, o_next, o_opp = slot_of(0, 1), slot_of(3, 1), slot_of(1, 1), slot_of(2, 1)

    def send(u, full):
        copy(XP, u, full, me_slot, x_next).start()
        copy(XM, u, full, me_slot, x_prev).start()
        copy(CO, u, full, me_slot, other).start()

    def forward(u, full):
        copy(XP, u, full, s_prev, x_next).wait_recv()
        copy(F0, u, full, s_prev, x_next, 0).start()
        copy(CXM, u, full, s_prev, other).start()
        copy(XM, u, full, s_next, x_prev).wait_recv()
        copy(F1, u, full, s_next, x_prev, 1).start()
        copy(CXP, u, full, s_next, other).start()

    def opposite(u, full):
        copy(F0, u, full, s_opp, x_next, 0).wait_recv()
        copy(C0, u, full, s_opp, other, 0).start()
        copy(F1, u, full, s_opp, x_prev, 1).wait_recv()
        copy(C1, u, full, s_opp, other, 1).start()

    def weights():
        for c in own_w[2:]:
            c.wait()
        for dx, dc in plane:
            for yb in range(2):
                w_copy(dx, dc, yb, 1, slot_of(NX - dx, dc)).wait_recv()
        for d in range(1, 4):
            z_copy(d, z_rows(4 - d)).wait_recv()

    def project(u, full):
        copy(CO, u, full, o_me, other).wait_recv()
        copy(CXM, u, full, o_prev, other).wait_recv()
        copy(CXP, u, full, o_next, other).wait_recv()
        copy(C0, u, full, o_opp, other, 0).wait_recv()
        copy(C1, u, full, o_opp, other, 1).wait_recv()
        n, lanes = lanes_of(u, full)

        def partial(yb):
            total = None
            for slot in range(SLOTS):
                term = lax.dot_general(
                    w[slot, yb], g[n, slot * CH : (slot + 1) * CH, lanes],
                    (((0,), (0,)), ((), ())), preferred_element_type=jnp.float32,
                )
                total = term if total is None else total + term
            return total

        ysend[n, :, lanes] = partial(1 - yh).astype(jnp.bfloat16)
        y_copy(u, full).start()
        pself[n, :, lanes] = partial(yh)

    def finish(u, full):
        y_copy(u, full).wait_recv()
        n, lanes = lanes_of(u, full)
        if full:
            ts = pl.ds(pl.multiple_of(n * CHUNK, CHUNK), CHUNK)
        else:
            ts = pl.ds(pl.multiple_of(u * LANES + (NC - 1) * LANES, LANES), LANES)
        out_ref[:, ts] = (pself[n, :, lanes] + yrecv[n, :, lanes].astype(jnp.float32)).astype(jnp.bfloat16)

    def turn(i, c0):
        @pl.when(i < NC)
        def _():
            conv(i)

        def at(lag, f):
            u = i - lag

            @pl.when(jnp.logical_and(u >= 0, u < NC - 1))
            def _():
                f(u, True)

            @pl.when(jnp.logical_and(u >= NC - 1, u < NU))
            def _():
                f(u, False)

        at(0, send)
        at(LAG_FWD, forward)
        at(LAG_OPP, opposite)

        @pl.when(i == LAG_MM)
        def _():
            weights()

        at(LAG_MM, project)
        at(LAG_FIN, finish)
        return c0

    lax.fori_loop(0, NU + LAG_FIN, turn, 0)

    def drain(full):
        def body(u, c0):
            copy(XP, u, full, me_slot, x_next).wait_send()
            copy(XM, u, full, me_slot, x_prev).wait_send()
            copy(CO, u, full, me_slot, other).wait_send()
            copy(F0, u, full, s_prev, x_next, 0).wait_send()
            copy(F1, u, full, s_next, x_prev, 1).wait_send()
            copy(CXM, u, full, s_prev, other).wait_send()
            copy(CXP, u, full, s_next, other).wait_send()
            copy(C0, u, full, s_opp, other, 0).wait_send()
            copy(C1, u, full, s_opp, other, 1).wait_send()
            y_copy(u, full).wait_send()
            return c0

        return body

    lax.fori_loop(0, NC - 1, drain(True), 0)
    lax.fori_loop(NC - 1, NU, drain(False), 0)
    for dx, dc in plane:
        for yb in range(2):
            for part in range(2):
                w_copy(dx, dc, yb, part, me_slot).wait_send()
    for d in range(1, 4):
        z_copy(d, z_rows(0)).wait_send()
    for d in range(1, CTX):
        state_copy(d, ctx).wait_send()


def on_device(key_feature, value_feature, query_gate, decay_rates, residues, skip_gain, out_weight):
    anywhere = pl.BlockSpec(memory_space=pl.ANY)
    local = pl.BlockSpec(memory_space=pltpu.VMEM)
    bf16, f32 = jnp.bfloat16, jnp.float32
    return pl.pallas_call(
        kernel,
        out_shape=pltpu.VMEM((CH, TOK), bf16),
        in_specs=[anywhere, anywhere, anywhere, local, local, local, anywhere],
        out_specs=local,
        scratch_shapes=[
            pltpu.VMEM((CH, TOK), bf16),
            pltpu.VMEM((CH, TOK), bf16),
            pltpu.VMEM((CH, TOK), bf16),
            pltpu.VMEM((CH // LANES, TOK // SUB * PITCH, LANES), f32),
            pltpu.VMEM((NC, MODES, 8, CH), f32),
            pltpu.VMEM((NC, MODES, CH), f32),
            pltpu.VMEM((MODES, 8, CH), f32),
            pltpu.VMEM((MODES, 8, CH), f32),
            pltpu.VMEM((MODES, 8, CH), f32),
            pltpu.VMEM((MODES, 8, CH), f32),
            pltpu.VMEM((3, MODES, CH), f32),
            pltpu.VMEM((MODES, CH), f32),
            pltpu.VMEM((CTX, MODES, CH), f32),
            pltpu.VMEM((NC, SLOTS * CH, CHUNK), bf16),
            pltpu.VMEM((SLOTS, 2, CH, CH), bf16),
            pltpu.VMEM((NC, CH, CHUNK), f32),
            pltpu.VMEM((NC, CH, CHUNK), bf16),
            pltpu.VMEM((NC, CH, CHUNK), bf16),
            pltpu.SemaphoreType.DMA((7,)),
            pltpu.SemaphoreType.DMA((10, NU)),
            pltpu.SemaphoreType.DMA((10, NU)),
            pltpu.SemaphoreType.DMA((CTX,)),
            pltpu.SemaphoreType.DMA((CTX,)),
            pltpu.SemaphoreType.DMA((SLOTS, 2, 2)),
            pltpu.SemaphoreType.DMA((SLOTS, 2, 2)),
            pltpu.SemaphoreType.DMA((4,)),
            pltpu.SemaphoreType.DMA((4,)),
        ],
        compiler_params=pltpu.CompilerParams(
            collective_id=0, has_side_effects=True, vmem_limit_bytes=56 * 2**20
        ),
        name="hyena",
    )(
        key_feature, value_feature, query_gate, decay_rates, residues,
        skip_gain.reshape(1, CH), out_weight,
    )


def solution(mesh):
    return jax.shard_map(
        on_device,
        mesh=mesh,
        in_specs=(
            P("tp", "ctx"), P("tp", "ctx"), P("tp", "ctx"),
            P(None, "tp"), P(None, "tp"), P("tp"), P("tp", None),
        ),
        out_specs=P("tp", "ctx"),
        check_vma=False,
    )
```

```python
import functools

import jax
import jax.numpy as jnp
from jax import lax
from jax.experimental import pallas as pl
from jax.experimental.pallas import tpu as pltpu
from jax.sharding import PartitionSpec as P

MESH = pl.DeviceIdType.MESH

MODES = 16
CH = 256
TOK = 2048
CHUNK = 256
NC = TOK // CHUNK
NU = NC + 1
SUB = 32
PITCH = 40
LANES = 128
CTX = 8
NX = 4
SLOTS = 8
W_Z = 128

XP, XM, CO, F0, F1, CXM, CXP, C0, C1, YY = range(10)
TURNS = NU + 4
EARLY = 0


def kernel(
    key_hbm, val_hbm, gate_hbm, rate_ref, res_ref, skip_ref, w_hbm, out_ref,
    keyb, valb, gateb, xt, est, gtot, am1, am2, am4, apow, coef, carry, fr,
    g, w, pself, ysend, yrecv,
    in_sem, ss, rs, fss, frs, wss, wrs, zss, zrs, ready_sem,
):
    ctx = lax.axis_index("ctx")
    tp = lax.axis_index("tp")
    x = tp // 4
    yh = (tp // 2) % 2
    core = tp % 2

    def dev(dx, dy, dc):
        return (ctx, ((x + dx) % NX) * 4 + ((yh + dy) % 2) * 2 + (core + dc) % 2)

    z = ctx % 4
    y_lo = ctx // 4

    def peer(dy, dz):
        return (((y_lo + dy) % 2) * 4 + (z + dz) % 4, tp)

    along = [(dy, dz) for dy in range(2) for dz in range(4) if (dy, dz) != (0, 0)]

    x_next, x_prev, other, y_dev = dev(1, 0, 0), dev(3, 0, 0), dev(0, 0, 1), dev(0, 1, 0)
    plane = [(dx, dc) for dx in range(NX) for dc in range(2) if (dx, dc) != (0, 0)]

    barrier = pltpu.get_barrier_semaphore()
    for dx, dc in plane:
        pl.semaphore_signal(barrier, inc=1, device_id=dev(dx, 0, dc), device_id_type=MESH)
    pl.semaphore_signal(barrier, inc=1, device_id=y_dev, device_id_type=MESH)
    pl.semaphore_signal(barrier, inc=1, device_id=peer(1, 0), device_id_type=MESH)
    for dy in range(2):
        for dz in range(1, 4):

            @pl.when(z + dz < 4)
            def _():
                pl.semaphore_signal(barrier, inc=1, device_id=peer(dy, dz), device_id_type=MESH)

    loads = [
        pltpu.make_async_copy(key_hbm, keyb, in_sem.at[0]),
        pltpu.make_async_copy(val_hbm, valb, in_sem.at[1]),
        pltpu.make_async_copy(gate_hbm, gateb, in_sem.at[2]),
    ]
    for c in loads:
        c.start()

    def slot_of(dx, dc):
        return ((x + dx) % NX) * 2 + (core + dc) % 2

    me_slot = slot_of(0, 0)

    def z_rows(d):
        return pl.ds(pl.multiple_of(((z + d) % 4) * (W_Z // 4), 16), W_Z // 4)

    def y_rows(d):
        half = (CH - W_Z) // 2
        return pl.ds(pl.multiple_of(W_Z + ((y_lo + d) % 2) * half, 16), half)

    w_rows = (z_rows(0), y_rows(0))

    def w_cols(dx, dc, yb, part):
        col = (((x + dx) % NX) * 4 + yb * 2 + (core + dc) % 2) * CH
        return w_hbm.at[w_rows[part], pl.ds(pl.multiple_of(col, CH), CH)]

    own_w = [
        pltpu.make_async_copy(
            w_cols(0, 0, yb, part), w.at[me_slot, yb, w_rows[part]], in_sem.at[3 + part * 2 + yb]
        )
        for part in range(2)
        for yb in range(2)
    ]
    for c in own_w:
        c.start()

    def w_copy(dx, dc, yb, part, slot):
        i = dx * 2 + dc
        return pltpu.make_async_remote_copy(
            w_cols(dx, dc, yb, part), w.at[slot, yb, w_rows[part]], wss.at[i, yb, part], wrs.at[i, yb, part],
            device_id=dev(dx, 0, dc), device_id_type=MESH,
        )

    def share_copy(d, rows):
        part = w.at[:, :, rows, :]
        return pltpu.make_async_remote_copy(
            part, part, zss.at[d], zrs.at[d], device_id=peer(d // 4, d % 4), device_id_type=MESH
        )

    rate = rate_ref[...]
    for m in range(MODES):
        r8 = jnp.broadcast_to(rate[m : m + 1, :], (8, CH))
        sub = lax.broadcasted_iota(jnp.int32, (8, CH), 0)
        subf = sub.astype(jnp.float32)
        am1[m] = jnp.where(sub >= 1, jnp.exp(-r8 * float(SUB)), 0.0)
        am2[m] = jnp.where(sub >= 2, jnp.exp(-r8 * float(2 * SUB)), 0.0)
        am4[m] = jnp.where(sub >= 4, jnp.exp(-r8 * float(4 * SUB)), 0.0)
        apow[m] = jnp.exp(-r8 * (subf * float(SUB)))
    coef[0] = jnp.exp(-rate)
    coef[1] = res_ref[...] * jnp.sqrt(2.0 * rate / MODES)
    coef[2] = jnp.exp(-rate * float(CHUNK))

    loads[0].wait()
    loads[1].wait()

    def sub_rows(n, q):
        return pl.ds(pl.multiple_of((n * 8 + q) * PITCH, 8), SUB)

    def step_rows(n, i):
        return pl.ds(n * (8 * PITCH) + i, 8, stride=PITCH)

    def pass1(n, c0):
        ts = pl.ds(pl.multiple_of(n * CHUNK, CHUNK), CHUNK)
        prod = (keyb[:, ts].astype(jnp.float32) * valb[:, ts].astype(jnp.float32)).astype(jnp.bfloat16)
        prod = prod.astype(jnp.float32).T
        for h in range(CH // LANES):
            for q in range(8):
                xt[h, sub_rows(n, q), :] = prod[q * SUB : (q + 1) * SUB, h * LANES : (h + 1) * LANES]
        for h in range(CH // LANES):
            ls = slice(h * LANES, (h + 1) * LANES)
            a = [jnp.broadcast_to(coef[0, m : m + 1, ls], (8, LANES)) for m in range(MODES)]

            hs = [jnp.zeros((8, LANES), jnp.float32)] * MODES
            for i in range(SUB):
                xv = xt[h, step_rows(n, i), :]
                hs = [a[m] * hs[m] + xv for m in range(MODES)]
            first = lax.broadcasted_iota(jnp.int32, (8, LANES), 0) == 0
            for m in range(MODES):
                s = hs[m]
                s = s + am1[m, :, ls] * pltpu.roll(s, 1, 0)
                s = s + am2[m, :, ls] * pltpu.roll(s, 2, 0)
                s = s + am4[m, :, ls] * pltpu.roll(s, 4, 0)
                est[n, m, :, ls] = jnp.where(first, 0.0, pltpu.roll(s, 1, 0))
                gtot[n, m : m + 1, ls] = s[7:8, :]
        return c0

    lax.fori_loop(0, EARLY, pass1, 0)
    pl.semaphore_wait(barrier, len(plane) + 2 + 2 * z)
    for dy in range(2):
        for dz in range(1, 4):

            @pl.when(z >= dz)
            def _():
                pl.semaphore_signal(
                    ready_sem.at[dz], inc=1, device_id=peer(dy, 4 - dz), device_id_type=MESH
                )

    for part in range(2):
        for dx, dc in plane:
            for yb in range(2):
                w_copy(dx, dc, yb, part, me_slot).start()

    lax.fori_loop(EARLY, NC, pass1, 0)

    final = jnp.zeros((MODES, CH), jnp.float32)
    for n in range(NC):
        final = coef[2] * final + gtot[n]
    fr[ctx] = final

    def state_copy(dy, dz, slot):
        i = dy * 4 + dz
        return pltpu.make_async_remote_copy(
            fr.at[slot], fr.at[slot], fss.at[i], frs.at[i], device_id=peer(dy, dz), device_id_type=MESH
        )

    def goes(dy, dz):
        up = z + dz < 4
        return (up if dz else False) if dy == 0 else y_lo == 0

    def higher(dz):
        @pl.when(z + dz < 4)
        def _():
            pl.semaphore_wait(ready_sem.at[dz], 2)
            state_copy(0, dz, ctx).start()

            @pl.when(y_lo == 0)
            def _():
                state_copy(1, dz, ctx).start()

    for dz in range(4):

        @pl.when(jnp.logical_and(y_lo == 0, jnp.logical_or(dz == 0, z + dz >= 4)))
        def _():
            state_copy(1, dz, ctx).start()

    for dz in range(1, 4):
        higher(dz)

    def share(part):
        for c in own_w[2 * part : 2 * part + 2]:
            c.wait()
        for dx, dc in plane:
            for yb in range(2):
                w_copy(dx, dc, yb, part, slot_of(NX - dx, dc)).wait_recv()
        if part == 0:
            for d in range(1, 4):
                share_copy(d, z_rows(0)).start()
        else:
            share_copy(4, y_rows(0)).start()

    share(0)
    loads[2].wait()
    carry[...] = jnp.zeros((MODES, CH), jnp.float32)
    for dy, dz in along:

        @pl.when(z >= dz if dy == 0 else y_lo == 1)
        def _():
            slot = ((y_lo + dy) % 2) * 4 + (z + 4 - dz) % 4
            state_copy(dy, dz, slot).wait_recv()
            gap = dz - 1 if dy == 0 else jnp.where(z >= dz, dz + 3, dz - 1)
            gap = jnp.asarray(gap, jnp.int32).astype(jnp.float32) * float(TOK)
            carry[...] += jnp.exp(-rate_ref[...] * gap) * fr[slot]

    def conv(n):
        for h in range(CH // LANES):
            ls = slice(h * LANES, (h + 1) * LANES)
            a = [jnp.broadcast_to(coef[0, m : m + 1, ls], (8, LANES)) for m in range(MODES)]
            b = [jnp.broadcast_to(coef[1, m : m + 1, ls], (8, LANES)) for m in range(MODES)]
            skip = jnp.broadcast_to(skip_ref[:, ls], (8, LANES))

            hs = [est[n, m, :, ls] + apow[m, :, ls] * carry[m : m + 1, ls] for m in range(MODES)]
            for i in range(SUB):
                at = step_rows(n, i)
                xv = xt[h, at, :]
                hs = [a[m] * hs[m] + xv for m in range(MODES)]
                terms = [skip * xv] + [b[m] * hs[m] for m in range(MODES)]
                while len(terms) > 1:
                    terms = [
                        terms[q] + terms[q + 1] if q + 1 < len(terms) else terms[q]
                        for q in range(0, len(terms), 2)
                    ]
                xt[h, at, :] = terms[0]
        carry[...] = coef[2] * carry[...] + gtot[n]
        ts = pl.ds(pl.multiple_of(n * CHUNK, CHUNK), CHUNK)
        for h in range(CH // LANES):
            filtered = jnp.concatenate([xt[h, sub_rows(n, q), :] for q in range(8)], axis=0).T
            rows = pl.ds(pl.multiple_of(me_slot * CH + h * LANES, LANES), LANES)
            gate = gateb[h * LANES : (h + 1) * LANES, ts].astype(jnp.float32)
            g[n, rows, :] = (gate * filtered).astype(jnp.bfloat16)

    def lanes_of(u, full):
        if full:
            return u, pl.ds(0, CHUNK)
        return NC - 1, pl.ds(pl.multiple_of((u - (NC - 1)) * LANES, LANES), LANES)

    def copy(kind, u, full, slot, device, half=None):
        n, lanes = lanes_of(u, full)
        first = slot * CH + (0 if half is None else half * (CH // 2))
        size = CH if half is None else CH // 2
        ref = g.at[n, pl.ds(pl.multiple_of(first, size), size), lanes]
        return pltpu.make_async_remote_copy(
            ref, ref, ss.at[kind, u], rs.at[kind, u], device_id=device, device_id_type=MESH
        )

    def y_copy(u, full):
        n, lanes = lanes_of(u, full)
        return pltpu.make_async_remote_copy(
            ysend.at[n, :, lanes], yrecv.at[n, :, lanes], ss.at[YY, u], rs.at[YY, u],
            device_id=y_dev, device_id_type=MESH,
        )

    s_prev, s_next, s_opp = slot_of(3, 0), slot_of(1, 0), slot_of(2, 0)
    o_me, o_prev, o_next, o_opp = slot_of(0, 1), slot_of(3, 1), slot_of(1, 1), slot_of(2, 1)

    def send(u, full):
        copy(XP, u, full, me_slot, x_next).start()
        copy(XM, u, full, me_slot, x_prev).start()
        copy(CO, u, full, me_slot, other).start()

    def forward(u, full):
        copy(XP, u, full, s_prev, x_next).wait_recv()
        copy(F0, u, full, s_prev, x_next, 0).start()
        copy(CXM, u, full, s_prev, other).start()
        copy(XM, u, full, s_next, x_prev).wait_recv()
        copy(F1, u, full, s_next, x_prev, 1).start()
        copy(CXP, u, full, s_next, other).start()

    def opposite(u, full):
        copy(F0, u, full, s_opp, x_next, 0).wait_recv()
        copy(C0, u, full, s_opp, other, 0).start()
        copy(F1, u, full, s_opp, x_prev, 1).wait_recv()
        copy(C1, u, full, s_opp, other, 1).start()

    def weights():
        for d in range(1, 4):
            share_copy(d, z_rows(4 - d)).wait_recv()
        share_copy(4, y_rows(1)).wait_recv()

    def project(u, full):
        copy(CO, u, full, o_me, other).wait_recv()
        copy(CXM, u, full, o_prev, other).wait_recv()
        copy(CXP, u, full, o_next, other).wait_recv()
        copy(C0, u, full, o_opp, other, 0).wait_recv()
        copy(C1, u, full, o_opp, other, 1).wait_recv()
        n, lanes = lanes_of(u, full)

        def partial(yb):
            total = None
            for slot in range(SLOTS):
                term = lax.dot_general(
                    w[slot, yb], g[n, slot * CH : (slot + 1) * CH, lanes],
                    (((0,), (0,)), ((), ())), preferred_element_type=jnp.float32,
                )
                total = term if total is None else total + term
            return total

        ysend[n, :, lanes] = partial(1 - yh).astype(jnp.bfloat16)
        y_copy(u, full).start()
        pself[n, :, lanes] = partial(yh)

    def finish(u, full):
        y_copy(u, full).wait_recv()
        n, lanes = lanes_of(u, full)
        if full:
            ts = pl.ds(pl.multiple_of(n * CHUNK, CHUNK), CHUNK)
        else:
            ts = pl.ds(pl.multiple_of(u * LANES + (NC - 1) * LANES, LANES), LANES)
        out_ref[:, ts] = (pself[n, :, lanes] + yrecv[n, :, lanes].astype(jnp.float32)).astype(jnp.bfloat16)

    def drain(u, full):
        copy(XP, u, full, me_slot, x_next).wait_send()
        copy(XM, u, full, me_slot, x_prev).wait_send()
        copy(CO, u, full, me_slot, other).wait_send()
        copy(F0, u, full, s_prev, x_next, 0).wait_send()
        copy(F1, u, full, s_next, x_prev, 1).wait_send()
        copy(CXM, u, full, s_prev, other).wait_send()
        copy(CXP, u, full, s_next, other).wait_send()
        copy(C0, u, full, s_opp, other, 0).wait_send()
        copy(C1, u, full, s_opp, other, 1).wait_send()
        y_copy(u, full).wait_send()

    def drain_start():
        for dx, dc in plane:
            for yb in range(2):
                for part in range(2):
                    w_copy(dx, dc, yb, part, me_slot).wait_send()
        for d in range(1, 4):
            share_copy(d, z_rows(0)).wait_send()
        share_copy(4, y_rows(0)).wait_send()
        for dy, dz in along:

            @pl.when(goes(dy, dz))
            def _():
                state_copy(dy, dz, ctx).wait_send()

    def turn(i, c0):
        @pl.when(i < NC)
        def _():
            conv(i)

        def at(lag, f, first=0, end=NU):
            u = i - lag
            for lo, hi, full in ((first, min(end, NC - 1), True), (max(first, NC - 1), end, False)):
                if lo < hi:

                    @pl.when(jnp.logical_and(u >= lo, u < hi))
                    def _():
                        f(u, full)

        at(0, send)
        at(1, forward)
        at(2, opposite)

        @pl.when(i == 1)
        def _():
            share(1)

        @pl.when(i == 4)
        def _():
            weights()

        at(4, project, 0, 2)
        at(3, project, 2, NU)
        at(6, finish, 0, 2)
        at(5, finish, 2, NC - 1)
        at(4, finish, NC - 1, NU)
        at(7, drain, 0, TURNS - 7)

        @pl.when(i == 6)
        def _():
            drain_start()

        return c0

    lax.fori_loop(0, TURNS, turn, 0)

    def drain_rest(u, c0):
        drain(u, True)
        return c0

    lax.fori_loop(TURNS - 7, NC - 1, drain_rest, 0)
    for u in range(NC - 1, NU):
        drain(u, False)


def on_device(key_feature, value_feature, query_gate, decay_rates, residues, skip_gain, out_weight):
    anywhere = pl.BlockSpec(memory_space=pl.ANY)
    local = pl.BlockSpec(memory_space=pltpu.VMEM)
    bf16, f32 = jnp.bfloat16, jnp.float32
    return pl.pallas_call(
        kernel,
        out_shape=pltpu.VMEM((CH, TOK), bf16),
        in_specs=[anywhere, anywhere, anywhere, local, local, local, anywhere],
        out_specs=local,
        scratch_shapes=[
            pltpu.VMEM((CH, TOK), bf16),
            pltpu.VMEM((CH, TOK), bf16),
            pltpu.VMEM((CH, TOK), bf16),
            pltpu.VMEM((CH // LANES, TOK // SUB * PITCH, LANES), f32),
            pltpu.VMEM((NC, MODES, 8, CH), f32),
            pltpu.VMEM((NC, MODES, CH), f32),
            pltpu.VMEM((MODES, 8, CH), f32),
            pltpu.VMEM((MODES, 8, CH), f32),
            pltpu.VMEM((MODES, 8, CH), f32),
            pltpu.VMEM((MODES, 8, CH), f32),
            pltpu.VMEM((3, MODES, CH), f32),
            pltpu.VMEM((MODES, CH), f32),
            pltpu.VMEM((CTX, MODES, CH), f32),
            pltpu.VMEM((NC, SLOTS * CH, CHUNK), bf16),
            pltpu.VMEM((SLOTS, 2, CH, CH), bf16),
            pltpu.VMEM((NC, CH, CHUNK), f32),
            pltpu.VMEM((NC, CH, CHUNK), bf16),
            pltpu.VMEM((NC, CH, CHUNK), bf16),
            pltpu.SemaphoreType.DMA((7,)),
            pltpu.SemaphoreType.DMA((10, NU)),
            pltpu.SemaphoreType.DMA((10, NU)),
            pltpu.SemaphoreType.DMA((CTX,)),
            pltpu.SemaphoreType.DMA((CTX,)),
            pltpu.SemaphoreType.DMA((SLOTS, 2, 2)),
            pltpu.SemaphoreType.DMA((SLOTS, 2, 2)),
            pltpu.SemaphoreType.DMA((5,)),
            pltpu.SemaphoreType.DMA((5,)),
            pltpu.SemaphoreType.REGULAR((4,)),
        ],
        compiler_params=pltpu.CompilerParams(
            collective_id=0, has_side_effects=True, vmem_limit_bytes=56 * 2**20
        ),
        name="hyena",
    )(
        key_feature, value_feature, query_gate, decay_rates, residues,
        skip_gain.reshape(1, CH), out_weight,
    )


def solution(mesh):
    return jax.shard_map(
        on_device,
        mesh=mesh,
        in_specs=(
            P("tp", "ctx"), P("tp", "ctx"), P("tp", "ctx"),
            P(None, "tp"), P(None, "tp"), P("tp"), P("tp", None),
        ),
        out_specs=P("tp", "ctx"),
        check_vma=False,
    )
```

```python
import functools

import jax
import jax.numpy as jnp
from jax import lax
from jax.experimental import pallas as pl
from jax.experimental.pallas import tpu as pltpu
from jax.sharding import PartitionSpec as P

MESH = pl.DeviceIdType.MESH

MODES = 16
CH = 256
TOK = 2048
CHUNK = 256
NC = TOK // CHUNK
NU = NC + 1
SUB = 32
PITCH = 40
LANES = 128
CTX = 8
NX = 4
SLOTS = 8
W_Z = 128

XP, XM, CO, F0, F1, CXM, CXP, C0, C1, YY = range(10)
TURNS = NU + 4
EARLY = 0


def kernel(
    key_hbm, val_hbm, gate_hbm, rate_ref, res_ref, skip_ref, w_hbm, out_ref,
    keyb, valb, gateb, xt, est, gtot, am1, am2, am4, apow, coef, carry, fr,
    g, w, pself, ysend, yrecv,
    in_sem, ss, rs, fss, frs, wss, wrs, zss, zrs, ready_sem,
):
    ctx = lax.axis_index("ctx")
    tp = lax.axis_index("tp")
    x = tp // 4
    yh = (tp // 2) % 2
    core = tp % 2

    def dev(dx, dy, dc):
        return (ctx, ((x + dx) % NX) * 4 + ((yh + dy) % 2) * 2 + (core + dc) % 2)

    z = ctx % 4
    y_lo = ctx // 4

    def peer(dy, dz):
        return (((y_lo + dy) % 2) * 4 + (z + dz) % 4, tp)

    along = [(dy, dz) for dy in range(2) for dz in range(4) if (dy, dz) != (0, 0)]

    x_next, x_prev, other, y_dev = dev(1, 0, 0), dev(3, 0, 0), dev(0, 0, 1), dev(0, 1, 0)
    plane = [(dx, dc) for dx in range(NX) for dc in range(2) if (dx, dc) != (0, 0)]

    barrier = pltpu.get_barrier_semaphore()
    for dx, dc in plane:
        pl.semaphore_signal(barrier, inc=1, device_id=dev(dx, 0, dc), device_id_type=MESH)
    pl.semaphore_signal(barrier, inc=1, device_id=y_dev, device_id_type=MESH)
    pl.semaphore_signal(barrier, inc=1, device_id=peer(1, 0), device_id_type=MESH)
    for dy in range(2):
        for dz in range(1, 4):

            @pl.when(z + dz < 4)
            def _():
                pl.semaphore_signal(barrier, inc=1, device_id=peer(dy, dz), device_id_type=MESH)

    loads = [
        pltpu.make_async_copy(key_hbm, keyb, in_sem.at[0]),
        pltpu.make_async_copy(val_hbm, valb, in_sem.at[1]),
        pltpu.make_async_copy(gate_hbm, gateb, in_sem.at[2]),
    ]
    for c in loads:
        c.start()

    def slot_of(dx, dc):
        return ((x + dx) % NX) * 2 + (core + dc) % 2

    me_slot = slot_of(0, 0)

    def z_rows(d):
        return pl.ds(pl.multiple_of(((z + d) % 4) * (W_Z // 4), 16), W_Z // 4)

    def y_rows(d):
        half = (CH - W_Z) // 2
        return pl.ds(pl.multiple_of(W_Z + ((y_lo + d) % 2) * half, 16), half)

    w_rows = (z_rows(0), y_rows(0))

    def w_cols(dx, dc, yb, part):
        col = (((x + dx) % NX) * 4 + yb * 2 + (core + dc) % 2) * CH
        return w_hbm.at[w_rows[part], pl.ds(pl.multiple_of(col, CH), CH)]

    own_w = [
        pltpu.make_async_copy(
            w_cols(0, 0, yb, part), w.at[me_slot, yb, w_rows[part]], in_sem.at[3 + part * 2 + yb]
        )
        for part in range(2)
        for yb in range(2)
    ]
    for c in own_w:
        c.start()

    def w_copy(dx, dc, yb, part, slot):
        i = dx * 2 + dc
        return pltpu.make_async_remote_copy(
            w_cols(dx, dc, yb, part), w.at[slot, yb, w_rows[part]], wss.at[i, yb, part], wrs.at[i, yb, part],
            device_id=dev(dx, 0, dc), device_id_type=MESH,
        )

    def share_copy(d, rows):
        part = w.at[:, :, rows, :]
        return pltpu.make_async_remote_copy(
            part, part, zss.at[d], zrs.at[d], device_id=peer(d // 4, d % 4), device_id_type=MESH
        )

    rate = rate_ref[...]
    for m in range(MODES):
        r8 = jnp.broadcast_to(rate[m : m + 1, :], (8, CH))
        sub = lax.broadcasted_iota(jnp.int32, (8, CH), 0)
        subf = sub.astype(jnp.float32)
        am1[m] = jnp.where(sub >= 1, jnp.exp(-r8 * float(SUB)), 0.0)
        am2[m] = jnp.where(sub >= 2, jnp.exp(-r8 * float(2 * SUB)), 0.0)
        am4[m] = jnp.where(sub >= 4, jnp.exp(-r8 * float(4 * SUB)), 0.0)
        apow[m] = jnp.exp(-r8 * (subf * float(SUB)))
    coef[0] = jnp.exp(-rate)
    coef[1] = res_ref[...] * jnp.sqrt(2.0 * rate / MODES)
    coef[2] = jnp.exp(-rate * float(CHUNK))

    loads[0].wait()
    loads[1].wait()

    def sub_rows(n, q):
        return pl.ds(pl.multiple_of((n * 8 + q) * PITCH, 8), SUB)

    def step_rows(n, i):
        return pl.ds(n * (8 * PITCH) + i, 8, stride=PITCH)

    def pass1(n, c0):
        ts = pl.ds(pl.multiple_of(n * CHUNK, CHUNK), CHUNK)
        prod = (keyb[:, ts].astype(jnp.float32) * valb[:, ts].astype(jnp.float32)).astype(jnp.bfloat16)
        prod = prod.astype(jnp.float32).T
        for h in range(CH // LANES):
            for q in range(8):
                xt[h, sub_rows(n, q), :] = prod[q * SUB : (q + 1) * SUB, h * LANES : (h + 1) * LANES]
        for h in range(CH // LANES):
            ls = slice(h * LANES, (h + 1) * LANES)
            a = [jnp.broadcast_to(coef[0, m : m + 1, ls], (8, LANES)) for m in range(MODES)]

            hs = [jnp.zeros((8, LANES), jnp.float32)] * MODES
            for i in range(SUB):
                xv = xt[h, step_rows(n, i), :]
                hs = [a[m] * hs[m] + xv for m in range(MODES)]
            first = lax.broadcasted_iota(jnp.int32, (8, LANES), 0) == 0
            for m in range(MODES):
                s = hs[m]
                s = s + am1[m, :, ls] * pltpu.roll(s, 1, 0)
                s = s + am2[m, :, ls] * pltpu.roll(s, 2, 0)
                s = s + am4[m, :, ls] * pltpu.roll(s, 4, 0)
                est[n, m, :, ls] = jnp.where(first, 0.0, pltpu.roll(s, 1, 0))
                gtot[n, m : m + 1, ls] = s[7:8, :]
        return c0

    lax.fori_loop(0, EARLY, pass1, 0)
    pl.semaphore_wait(barrier, len(plane) + 2 + 2 * z)
    for dy in range(2):
        for dz in range(1, 4):

            @pl.when(z >= dz)
            def _():
                pl.semaphore_signal(
                    ready_sem.at[dz], inc=1, device_id=peer(dy, 4 - dz), device_id_type=MESH
                )

    for part in range(2):
        for dx, dc in plane:
            for yb in range(2):
                w_copy(dx, dc, yb, part, me_slot).start()

    lax.fori_loop(EARLY, NC, pass1, 0)

    final = jnp.zeros((MODES, CH), jnp.float32)
    for n in range(NC):
        final = coef[2] * final + gtot[n]
    fr[ctx] = final

    def state_copy(dy, dz, slot):
        i = dy * 4 + dz
        return pltpu.make_async_remote_copy(
            fr.at[slot], fr.at[slot], fss.at[i], frs.at[i], device_id=peer(dy, dz), device_id_type=MESH
        )

    def goes(dy, dz):
        up = z + dz < 4
        return (up if dz else False) if dy == 0 else y_lo == 0

    def higher(dz):
        @pl.when(z + dz < 4)
        def _():
            pl.semaphore_wait(ready_sem.at[dz], 2)
            state_copy(0, dz, ctx).start()

            @pl.when(y_lo == 0)
            def _():
                state_copy(1, dz, ctx).start()

    for dz in range(4):

        @pl.when(jnp.logical_and(y_lo == 0, jnp.logical_or(dz == 0, z + dz >= 4)))
        def _():
            state_copy(1, dz, ctx).start()

    for dz in range(1, 4):
        higher(dz)

    def share(part):
        for c in own_w[2 * part : 2 * part + 2]:
            c.wait()
        for dx, dc in plane:
            for yb in range(2):
                w_copy(dx, dc, yb, part, slot_of(NX - dx, dc)).wait_recv()
        if part == 0:
            for d in range(1, 4):
                share_copy(d, z_rows(0)).start()
        else:
            share_copy(4, y_rows(0)).start()

    share(0)
    loads[2].wait()
    carry[...] = jnp.zeros((MODES, CH), jnp.float32)
    for dy, dz in along:

        @pl.when(z >= dz if dy == 0 else y_lo == 1)
        def _():
            slot = ((y_lo + dy) % 2) * 4 + (z + 4 - dz) % 4
            state_copy(dy, dz, slot).wait_recv()
            gap = dz - 1 if dy == 0 else jnp.where(z >= dz, dz + 3, dz - 1)
            gap = jnp.asarray(gap, jnp.int32).astype(jnp.float32) * float(TOK)
            carry[...] += jnp.exp(-rate_ref[...] * gap) * fr[slot]

    def conv(n):
        for h in range(CH // LANES):
            ls = slice(h * LANES, (h + 1) * LANES)
            a = [jnp.broadcast_to(coef[0, m : m + 1, ls], (8, LANES)) for m in range(MODES)]
            b = [jnp.broadcast_to(coef[1, m : m + 1, ls], (8, LANES)) for m in range(MODES)]
            skip = jnp.broadcast_to(skip_ref[:, ls], (8, LANES))

            hs = [est[n, m, :, ls] + apow[m, :, ls] * carry[m : m + 1, ls] for m in range(MODES)]
            for i in range(SUB):
                at = step_rows(n, i)
                xv = xt[h, at, :]
                hs = [a[m] * hs[m] + xv for m in range(MODES)]
                terms = [skip * xv] + [b[m] * hs[m] for m in range(MODES)]
                while len(terms) > 1:
                    terms = [
                        terms[q] + terms[q + 1] if q + 1 < len(terms) else terms[q]
                        for q in range(0, len(terms), 2)
                    ]
                xt[h, at, :] = terms[0]
        carry[...] = coef[2] * carry[...] + gtot[n]
        ts = pl.ds(pl.multiple_of(n * CHUNK, CHUNK), CHUNK)
        for h in range(CH // LANES):
            filtered = jnp.concatenate([xt[h, sub_rows(n, q), :] for q in range(8)], axis=0).T
            rows = pl.ds(pl.multiple_of(me_slot * CH + h * LANES, LANES), LANES)
            gate = gateb[h * LANES : (h + 1) * LANES, ts].astype(jnp.float32)
            g[n, rows, :] = (gate * filtered).astype(jnp.bfloat16)

    def lanes_of(u, full):
        if full:
            return u, pl.ds(0, CHUNK)
        return NC - 1, pl.ds(pl.multiple_of((u - (NC - 1)) * LANES, LANES), LANES)

    def copy(kind, u, full, slot, device, half=None):
        n, lanes = lanes_of(u, full)
        first = slot * CH + (0 if half is None else half * (CH // 2))
        size = CH if half is None else CH // 2
        ref = g.at[n, pl.ds(pl.multiple_of(first, size), size), lanes]
        return pltpu.make_async_remote_copy(
            ref, ref, ss.at[kind, u], rs.at[kind, u], device_id=device, device_id_type=MESH
        )

    def y_copy(u, full):
        n, lanes = lanes_of(u, full)
        return pltpu.make_async_remote_copy(
            ysend.at[n, :, lanes], yrecv.at[n, :, lanes], ss.at[YY, u], rs.at[YY, u],
            device_id=y_dev, device_id_type=MESH,
        )

    s_prev, s_next, s_opp = slot_of(3, 0), slot_of(1, 0), slot_of(2, 0)
    o_me, o_prev, o_next, o_opp = slot_of(0, 1), slot_of(3, 1), slot_of(1, 1), slot_of(2, 1)

    def send(u, full):
        copy(XP, u, full, me_slot, x_next).start()
        copy(XM, u, full, me_slot, x_prev).start()
        copy(CO, u, full, me_slot, other).start()

    def forward(u, full):
        copy(XP, u, full, s_prev, x_next).wait_recv()
        copy(F0, u, full, s_prev, x_next, 0).start()
        copy(CXM, u, full, s_prev, other).start()
        copy(XM, u, full, s_next, x_prev).wait_recv()
        copy(F1, u, full, s_next, x_prev, 1).start()
        copy(CXP, u, full, s_next, other).start()

    def opposite(u, full):
        copy(F0, u, full, s_opp, x_next, 0).wait_recv()
        copy(C0, u, full, s_opp, other, 0).start()
        copy(F1, u, full, s_opp, x_prev, 1).wait_recv()
        copy(C1, u, full, s_opp, other, 1).start()

    def weights():
        for d in range(1, 4):
            share_copy(d, z_rows(4 - d)).wait_recv()
        share_copy(4, y_rows(1)).wait_recv()

    def project(u, full):
        copy(CO, u, full, o_me, other).wait_recv()
        copy(CXM, u, full, o_prev, other).wait_recv()
        copy(CXP, u, full, o_next, other).wait_recv()
        copy(C0, u, full, o_opp, other, 0).wait_recv()
        copy(C1, u, full, o_opp, other, 1).wait_recv()
        n, lanes = lanes_of(u, full)

        def partial(yb):
            total = None
            for slot in range(SLOTS):
                term = lax.dot_general(
                    w[slot, yb], g[n, slot * CH : (slot + 1) * CH, lanes],
                    (((0,), (0,)), ((), ())), preferred_element_type=jnp.float32,
                )
                total = term if total is None else total + term
            return total

        ysend[n, :, lanes] = partial(1 - yh).astype(jnp.bfloat16)
        y_copy(u, full).start()
        pself[n, :, lanes] = partial(yh)

    def finish(u, full):
        y_copy(u, full).wait_recv()
        n, lanes = lanes_of(u, full)
        if full:
            ts = pl.ds(pl.multiple_of(n * CHUNK, CHUNK), CHUNK)
        else:
            ts = pl.ds(pl.multiple_of(u * LANES + (NC - 1) * LANES, LANES), LANES)
        out_ref[:, ts] = (pself[n, :, lanes] + yrecv[n, :, lanes].astype(jnp.float32)).astype(jnp.bfloat16)

    def drain(u, full):
        copy(XP, u, full, me_slot, x_next).wait_send()
        copy(XM, u, full, me_slot, x_prev).wait_send()
        copy(CO, u, full, me_slot, other).wait_send()
        copy(F0, u, full, s_prev, x_next, 0).wait_send()
        copy(F1, u, full, s_next, x_prev, 1).wait_send()
        copy(CXM, u, full, s_prev, other).wait_send()
        copy(CXP, u, full, s_next, other).wait_send()
        copy(C0, u, full, s_opp, other, 0).wait_send()
        copy(C1, u, full, s_opp, other, 1).wait_send()
        if full or u < NU - 1:
            y_copy(u, full).wait_send()

    def drain_start():
        for dx, dc in plane:
            for yb in range(2):
                for part in range(2):
                    w_copy(dx, dc, yb, part, me_slot).wait_send()
        for d in range(1, 4):
            share_copy(d, z_rows(0)).wait_send()
        share_copy(4, y_rows(0)).wait_send()
        for dy, dz in along:

            @pl.when(goes(dy, dz))
            def _():
                state_copy(dy, dz, ctx).wait_send()

    def turn(i, c0):
        def at(lag, f, first=0, end=NU):
            u = i - lag
            for lo, hi, full in ((first, min(end, NC - 1), True), (max(first, NC - 1), end, False)):
                if lo < hi:

                    @pl.when(jnp.logical_and(u >= lo, u < hi))
                    def _():
                        f(u, full)

        at(0, send)
        at(1, forward)

        @pl.when(i == 1)
        def _():
            share(1)

        @pl.when(i == 4)
        def _():
            weights()

        at(4, project, 0, 2)
        at(3, project, 2, NU)
        at(6, finish, 0, 2)
        at(5, finish, 2, NC - 1)
        at(4, finish, NC - 1, NU - 1)

        @pl.when(i == TURNS - 1)
        def _():
            drain(NC - 2, True)
            for u in range(NC - 1, NU):
                drain(u, False)
            finish(NU - 1, False)


        @pl.when(i < NC - 1)
        def _():
            conv(i + 1)

        at(2, opposite)
        at(7, drain, 0, TURNS - 7)

        @pl.when(i == 6)
        def _():
            drain_start()

        return c0

    conv(0)
    lax.fori_loop(0, TURNS, turn, 0)

    y_copy(NU - 1, False).wait_send()


def on_device(key_feature, value_feature, query_gate, decay_rates, residues, skip_gain, out_weight):
    anywhere = pl.BlockSpec(memory_space=pl.ANY)
    local = pl.BlockSpec(memory_space=pltpu.VMEM)
    bf16, f32 = jnp.bfloat16, jnp.float32
    return pl.pallas_call(
        kernel,
        out_shape=pltpu.VMEM((CH, TOK), bf16),
        in_specs=[anywhere, anywhere, anywhere, local, local, local, anywhere],
        out_specs=local,
        scratch_shapes=[
            pltpu.VMEM((CH, TOK), bf16),
            pltpu.VMEM((CH, TOK), bf16),
            pltpu.VMEM((CH, TOK), bf16),
            pltpu.VMEM((CH // LANES, TOK // SUB * PITCH, LANES), f32),
            pltpu.VMEM((NC, MODES, 8, CH), f32),
            pltpu.VMEM((NC, MODES, CH), f32),
            pltpu.VMEM((MODES, 8, CH), f32),
            pltpu.VMEM((MODES, 8, CH), f32),
            pltpu.VMEM((MODES, 8, CH), f32),
            pltpu.VMEM((MODES, 8, CH), f32),
            pltpu.VMEM((3, MODES, CH), f32),
            pltpu.VMEM((MODES, CH), f32),
            pltpu.VMEM((CTX, MODES, CH), f32),
            pltpu.VMEM((NC, SLOTS * CH, CHUNK), bf16),
            pltpu.VMEM((SLOTS, 2, CH, CH), bf16),
            pltpu.VMEM((NC, CH, CHUNK), f32),
            pltpu.VMEM((NC, CH, CHUNK), bf16),
            pltpu.VMEM((NC, CH, CHUNK), bf16),
            pltpu.SemaphoreType.DMA((7,)),
            pltpu.SemaphoreType.DMA((10, NU)),
            pltpu.SemaphoreType.DMA((10, NU)),
            pltpu.SemaphoreType.DMA((CTX,)),
            pltpu.SemaphoreType.DMA((CTX,)),
            pltpu.SemaphoreType.DMA((SLOTS, 2, 2)),
            pltpu.SemaphoreType.DMA((SLOTS, 2, 2)),
            pltpu.SemaphoreType.DMA((5,)),
            pltpu.SemaphoreType.DMA((5,)),
            pltpu.SemaphoreType.REGULAR((4,)),
        ],
        compiler_params=pltpu.CompilerParams(
            collective_id=0, has_side_effects=True, vmem_limit_bytes=56 * 2**20
        ),
        name="hyena",
    )(
        key_feature, value_feature, query_gate, decay_rates, residues,
        skip_gain.reshape(1, CH), out_weight,
    )


def solution(mesh):
    return jax.shard_map(
        on_device,
        mesh=mesh,
        in_specs=(
            P("tp", "ctx"), P("tp", "ctx"), P("tp", "ctx"),
            P(None, "tp"), P(None, "tp"), P("tp"), P("tp", None),
        ),
        out_specs=P("tp", "ctx"),
        check_vma=False,
    )
```

```python
import functools

import jax
import jax.numpy as jnp
from jax import lax
from jax.experimental import pallas as pl
from jax.experimental.pallas import tpu as pltpu
from jax.sharding import PartitionSpec as P

MESH = pl.DeviceIdType.MESH

MODES = 16
CH = 256
TOK = 2048
CHUNK = 256
NC = TOK // CHUNK
NU = NC + 1
SUB = 32
PITCH = 40
LANES = 128
CTX = 8
NX = 4
SLOTS = 8
W_Z = 128

XP, XM, CO, F0, F1, CXM, CXP, C0, C1, YY = range(10)
TURNS = NU + 4


def kernel(
    key_hbm, val_hbm, gate_hbm, rate_ref, res_ref, skip_ref, w_hbm, out_ref,
    keyb, valb, gateb, xt, est, gtot, am1, am2, am4, apow, coef, carry, fr,
    g, w, pself, ysend, yrecv,
    in_sem, ss, rs, fss, frs, wss, wrs, zss, zrs, ready_sem,
):
    ctx = lax.axis_index("ctx")
    tp = lax.axis_index("tp")
    x = tp // 4
    yh = (tp // 2) % 2
    core = tp % 2

    def dev(dx, dy, dc):
        return (ctx, ((x + dx) % NX) * 4 + ((yh + dy) % 2) * 2 + (core + dc) % 2)

    z = ctx % 4
    y_lo = ctx // 4

    def peer(dy, dz):
        return (((y_lo + dy) % 2) * 4 + (z + dz) % 4, tp)

    along = [(dy, dz) for dy in range(2) for dz in range(4) if (dy, dz) != (0, 0)]

    x_next, x_prev, other, y_dev = dev(1, 0, 0), dev(3, 0, 0), dev(0, 0, 1), dev(0, 1, 0)
    plane = [(dx, dc) for dx in range(NX) for dc in range(2) if (dx, dc) != (0, 0)]

    barrier = pltpu.get_barrier_semaphore()
    for dx, dc in plane:
        pl.semaphore_signal(barrier, inc=1, device_id=dev(dx, 0, dc), device_id_type=MESH)
    pl.semaphore_signal(barrier, inc=1, device_id=y_dev, device_id_type=MESH)
    pl.semaphore_signal(barrier, inc=1, device_id=peer(1, 0), device_id_type=MESH)
    for dy in range(2):
        for dz in range(1, 4):

            @pl.when(z + dz < 4)
            def _():
                pl.semaphore_signal(barrier, inc=1, device_id=peer(dy, dz), device_id_type=MESH)

    loads = [
        pltpu.make_async_copy(key_hbm, keyb, in_sem.at[0]),
        pltpu.make_async_copy(val_hbm, valb, in_sem.at[1]),
        pltpu.make_async_copy(gate_hbm, gateb, in_sem.at[2]),
    ]
    for c in loads:
        c.start()

    def slot_of(dx, dc):
        return ((x + dx) % NX) * 2 + (core + dc) % 2

    me_slot = slot_of(0, 0)

    def z_rows(d):
        return pl.ds(pl.multiple_of(((z + d) % 4) * (W_Z // 4), 16), W_Z // 4)

    def y_rows(d):
        half = (CH - W_Z) // 2
        return pl.ds(pl.multiple_of(W_Z + ((y_lo + d) % 2) * half, 16), half)

    w_rows = (z_rows(0), y_rows(0))

    def w_cols(dx, dc, yb, part):
        col = (((x + dx) % NX) * 4 + yb * 2 + (core + dc) % 2) * CH
        return w_hbm.at[w_rows[part], pl.ds(pl.multiple_of(col, CH), CH)]

    own_w = [
        pltpu.make_async_copy(
            w_cols(0, 0, yb, part), w.at[me_slot, yb, w_rows[part]], in_sem.at[3 + part * 2 + yb]
        )
        for part in range(2)
        for yb in range(2)
    ]
    for c in own_w:
        c.start()

    def w_copy(dx, dc, yb, part, slot):
        i = dx * 2 + dc
        return pltpu.make_async_remote_copy(
            w_cols(dx, dc, yb, part), w.at[slot, yb, w_rows[part]], wss.at[i, yb, part], wrs.at[i, yb, part],
            device_id=dev(dx, 0, dc), device_id_type=MESH,
        )

    def share_copy(d, rows):
        part = w.at[:, :, rows, :]
        return pltpu.make_async_remote_copy(
            part, part, zss.at[d], zrs.at[d], device_id=peer(d // 4, d % 4), device_id_type=MESH
        )

    rate = rate_ref[...]
    for m in range(MODES):
        r8 = jnp.broadcast_to(rate[m : m + 1, :], (8, CH))
        sub = lax.broadcasted_iota(jnp.int32, (8, CH), 0)
        subf = sub.astype(jnp.float32)
        am1[m] = jnp.where(sub >= 1, jnp.exp(-r8 * float(SUB)), 0.0)
        am2[m] = jnp.where(sub >= 2, jnp.exp(-r8 * float(2 * SUB)), 0.0)
        am4[m] = jnp.where(sub >= 4, jnp.exp(-r8 * float(4 * SUB)), 0.0)
        apow[m] = jnp.exp(-r8 * (subf * float(SUB)))
    coef[0] = jnp.exp(-rate)
    coef[1] = res_ref[...] * jnp.sqrt(2.0 * rate / MODES)
    coef[2] = jnp.exp(-rate * float(CHUNK))

    loads[0].wait()
    loads[1].wait()

    def sub_rows(n, q):
        return pl.ds(pl.multiple_of((n * 8 + q) * PITCH, 8), SUB)

    def step_rows(n, i):
        return pl.ds(n * (8 * PITCH) + i, 8, stride=PITCH)

    def pass1(n, c0):
        ts = pl.ds(pl.multiple_of(n * CHUNK, CHUNK), CHUNK)
        prod = (keyb[:, ts].astype(jnp.float32) * valb[:, ts].astype(jnp.float32)).astype(jnp.bfloat16)
        prod = prod.astype(jnp.float32).T
        for h in range(CH // LANES):
            for q in range(8):
                xt[h, sub_rows(n, q), :] = prod[q * SUB : (q + 1) * SUB, h * LANES : (h + 1) * LANES]
        for h in range(CH // LANES):
            ls = slice(h * LANES, (h + 1) * LANES)
            a = [jnp.broadcast_to(coef[0, m : m + 1, ls], (8, LANES)) for m in range(MODES)]

            hs = [jnp.zeros((8, LANES), jnp.float32)] * MODES
            for i in range(SUB):
                xv = xt[h, step_rows(n, i), :]
                hs = [a[m] * hs[m] + xv for m in range(MODES)]
            first = lax.broadcasted_iota(jnp.int32, (8, LANES), 0) == 0
            for m in range(MODES):
                s = hs[m]
                s = s + am1[m, :, ls] * pltpu.roll(s, 1, 0)
                s = s + am2[m, :, ls] * pltpu.roll(s, 2, 0)
                s = s + am4[m, :, ls] * pltpu.roll(s, 4, 0)
                est[n, m, :, ls] = jnp.where(first, 0.0, pltpu.roll(s, 1, 0))
                gtot[n, m : m + 1, ls] = s[7:8, :]
        return c0

    pl.semaphore_wait(barrier, len(plane) + 2 + 2 * z)
    for dy in range(2):
        for dz in range(1, 4):

            @pl.when(z >= dz)
            def _():
                pl.semaphore_signal(
                    ready_sem.at[dz], inc=1, device_id=peer(dy, 4 - dz), device_id_type=MESH
                )

    for part in range(2):
        for dx, dc in plane:
            for yb in range(2):
                w_copy(dx, dc, yb, part, me_slot).start()

    def pass1_pair(k, c0):
        pass1(2 * k, c0)
        pass1(2 * k + 1, c0)
        return c0

    lax.fori_loop(0, NC // 2, pass1_pair, 0)

    final = jnp.zeros((MODES, CH), jnp.float32)
    for n in range(NC):
        final = coef[2] * final + gtot[n]
    fr[ctx] = final

    def state_copy(dy, dz, slot):
        i = dy * 4 + dz
        return pltpu.make_async_remote_copy(
            fr.at[slot], fr.at[slot], fss.at[i], frs.at[i], device_id=peer(dy, dz), device_id_type=MESH
        )

    def goes(dy, dz):
        up = z + dz < 4
        return (up if dz else False) if dy == 0 else y_lo == 0

    def higher(dz):
        @pl.when(z + dz < 4)
        def _():
            pl.semaphore_wait(ready_sem.at[dz], 2)
            state_copy(0, dz, ctx).start()

            @pl.when(y_lo == 0)
            def _():
                state_copy(1, dz, ctx).start()

    for dz in range(4):

        @pl.when(jnp.logical_and(y_lo == 0, jnp.logical_or(dz == 0, z + dz >= 4)))
        def _():
            state_copy(1, dz, ctx).start()

    for dz in range(1, 4):
        higher(dz)

    def share(part):
        for c in own_w[2 * part : 2 * part + 2]:
            c.wait()
        for dx, dc in plane:
            for yb in range(2):
                w_copy(dx, dc, yb, part, slot_of(NX - dx, dc)).wait_recv()
        if part == 0:
            for d in range(1, 4):
                share_copy(d, z_rows(0)).start()
        else:
            share_copy(4, y_rows(0)).start()

    share(0)
    loads[2].wait()
    carry[...] = jnp.zeros((MODES, CH), jnp.float32)
    for dy, dz in along:

        @pl.when(z >= dz if dy == 0 else y_lo == 1)
        def _():
            slot = ((y_lo + dy) % 2) * 4 + (z + 4 - dz) % 4
            state_copy(dy, dz, slot).wait_recv()
            gap = dz - 1 if dy == 0 else jnp.where(z >= dz, dz + 3, dz - 1)
            gap = jnp.asarray(gap, jnp.int32).astype(jnp.float32) * float(TOK)
            carry[...] += jnp.exp(-rate_ref[...] * gap) * fr[slot]

    def conv(n):
        for h in range(CH // LANES):
            ls = slice(h * LANES, (h + 1) * LANES)
            a = [jnp.broadcast_to(coef[0, m : m + 1, ls], (8, LANES)) for m in range(MODES)]
            b = [jnp.broadcast_to(coef[1, m : m + 1, ls], (8, LANES)) for m in range(MODES)]
            skip = jnp.broadcast_to(skip_ref[:, ls], (8, LANES))

            hs = [est[n, m, :, ls] + apow[m, :, ls] * carry[m : m + 1, ls] for m in range(MODES)]
            for i in range(SUB):
                at = step_rows(n, i)
                xv = xt[h, at, :]
                hs = [a[m] * hs[m] + xv for m in range(MODES)]
                terms = [skip * xv] + [b[m] * hs[m] for m in range(MODES)]
                while len(terms) > 1:
                    terms = [
                        terms[q] + terms[q + 1] if q + 1 < len(terms) else terms[q]
                        for q in range(0, len(terms), 2)
                    ]
                xt[h, at, :] = terms[0]
        carry[...] = coef[2] * carry[...] + gtot[n]
        ts = pl.ds(pl.multiple_of(n * CHUNK, CHUNK), CHUNK)
        for h in range(CH // LANES):
            filtered = jnp.concatenate([xt[h, sub_rows(n, q), :] for q in range(8)], axis=0).T
            rows = pl.ds(pl.multiple_of(me_slot * CH + h * LANES, LANES), LANES)
            gate = gateb[h * LANES : (h + 1) * LANES, ts].astype(jnp.float32)
            g[n, rows, :] = (gate * filtered).astype(jnp.bfloat16)

    def lanes_of(u, full):
        if full:
            return u, pl.ds(0, CHUNK)
        return NC - 1, pl.ds(pl.multiple_of((u - (NC - 1)) * LANES, LANES), LANES)

    def copy(kind, u, full, slot, device, half=None):
        n, lanes = lanes_of(u, full)
        first = slot * CH + (0 if half is None else half * (CH // 2))
        size = CH if half is None else CH // 2
        ref = g.at[n, pl.ds(pl.multiple_of(first, size), size), lanes]
        return pltpu.make_async_remote_copy(
            ref, ref, ss.at[kind, u], rs.at[kind, u], device_id=device, device_id_type=MESH
        )

    def y_copy(u, full):
        n, lanes = lanes_of(u, full)
        return pltpu.make_async_remote_copy(
            ysend.at[n, :, lanes], yrecv.at[n, :, lanes], ss.at[YY, u], rs.at[YY, u],
            device_id=y_dev, device_id_type=MESH,
        )

    s_prev, s_next, s_opp = slot_of(3, 0), slot_of(1, 0), slot_of(2, 0)
    o_me, o_prev, o_next, o_opp = slot_of(0, 1), slot_of(3, 1), slot_of(1, 1), slot_of(2, 1)

    def send(u, full):
        copy(XP, u, full, me_slot, x_next).start()
        copy(XM, u, full, me_slot, x_prev).start()
        copy(CO, u, full, me_slot, other).start()

    def forward(u, full):
        copy(XP, u, full, s_prev, x_next).wait_recv()
        copy(F0, u, full, s_prev, x_next, 0).start()
        copy(CXM, u, full, s_prev, other).start()
        copy(XM, u, full, s_next, x_prev).wait_recv()
        copy(F1, u, full, s_next, x_prev, 1).start()
        copy(CXP, u, full, s_next, other).start()

    def opposite(u, full):
        copy(F0, u, full, s_opp, x_next, 0).wait_recv()
        copy(C0, u, full, s_opp, other, 0).start()
        copy(F1, u, full, s_opp, x_prev, 1).wait_recv()
        copy(C1, u, full, s_opp, other, 1).start()

    def weights():
        for d in range(1, 4):
            share_copy(d, z_rows(4 - d)).wait_recv()
        share_copy(4, y_rows(1)).wait_recv()

    def project(u, full):
        copy(CO, u, full, o_me, other).wait_recv()
        copy(CXM, u, full, o_prev, other).wait_recv()
        copy(CXP, u, full, o_next, other).wait_recv()
        copy(C0, u, full, o_opp, other, 0).wait_recv()
        copy(C1, u, full, o_opp, other, 1).wait_recv()
        n, lanes = lanes_of(u, full)

        def partial(yb):
            total = None
            for slot in range(SLOTS):
                term = lax.dot_general(
                    w[slot, yb], g[n, slot * CH : (slot + 1) * CH, lanes],
                    (((0,), (0,)), ((), ())), preferred_element_type=jnp.float32,
                )
                total = term if total is None else total + term
            return total

        ysend[n, :, lanes] = partial(1 - yh).astype(jnp.bfloat16)
        y_copy(u, full).start()
        pself[n, :, lanes] = partial(yh)

    def finish(u, full):
        y_copy(u, full).wait_recv()
        n, lanes = lanes_of(u, full)
        if full:
            ts = pl.ds(pl.multiple_of(n * CHUNK, CHUNK), CHUNK)
        else:
            ts = pl.ds(pl.multiple_of(u * LANES + (NC - 1) * LANES, LANES), LANES)
        out_ref[:, ts] = (pself[n, :, lanes] + yrecv[n, :, lanes].astype(jnp.float32)).astype(jnp.bfloat16)

    def drain(u, full):
        copy(XP, u, full, me_slot, x_next).wait_send()
        copy(XM, u, full, me_slot, x_prev).wait_send()
        copy(CO, u, full, me_slot, other).wait_send()
        copy(F0, u, full, s_prev, x_next, 0).wait_send()
        copy(F1, u, full, s_next, x_prev, 1).wait_send()
        copy(CXM, u, full, s_prev, other).wait_send()
        copy(CXP, u, full, s_next, other).wait_send()
        copy(C0, u, full, s_opp, other, 0).wait_send()
        copy(C1, u, full, s_opp, other, 1).wait_send()
        if full or u < NU - 1:
            y_copy(u, full).wait_send()

    def drain_start():
        for dx, dc in plane:
            for yb in range(2):
                for part in range(2):
                    w_copy(dx, dc, yb, part, me_slot).wait_send()
        for d in range(1, 4):
            share_copy(d, z_rows(0)).wait_send()
        share_copy(4, y_rows(0)).wait_send()
        for dy, dz in along:

            @pl.when(goes(dy, dz))
            def _():
                state_copy(dy, dz, ctx).wait_send()

    def turn(i, c0):
        def at(lag, f, first=0, end=NU):
            u = i - lag
            for lo, hi, full in ((first, min(end, NC - 1), True), (max(first, NC - 1), end, False)):
                if lo < hi:

                    @pl.when(jnp.logical_and(u >= lo, u < hi))
                    def _():
                        f(u, full)

        at(0, send)
        at(1, forward)
        at(2, opposite, NC - 1, NU)

        @pl.when(i == 1)
        def _():
            share(1)

        @pl.when(i == 4)
        def _():
            weights()

        at(4, project, 0, 2)
        at(3, project, 2, NU)
        at(6, finish, 0, 2)
        at(5, finish, 2, NC - 1)
        at(4, finish, NC - 1, NU - 1)

        @pl.when(i == TURNS - 1)
        def _():
            drain(NC - 2, True)
            for u in range(NC - 1, NU):
                drain(u, False)
            finish(NU - 1, False)


        @pl.when(i < NC - 1)
        def _():
            conv(i + 1)

        at(2, opposite, 0, NC - 1)
        at(7, drain, 0, TURNS - 7)

        @pl.when(i == 6)
        def _():
            drain_start()

        return c0

    conv(0)
    lax.fori_loop(0, TURNS, turn, 0)

    y_copy(NU - 1, False).wait_send()


def on_device(key_feature, value_feature, query_gate, decay_rates, residues, skip_gain, out_weight):
    anywhere = pl.BlockSpec(memory_space=pl.ANY)
    local = pl.BlockSpec(memory_space=pltpu.VMEM)
    bf16, f32 = jnp.bfloat16, jnp.float32
    return pl.pallas_call(
        kernel,
        out_shape=pltpu.VMEM((CH, TOK), bf16),
        in_specs=[anywhere, anywhere, anywhere, local, local, local, anywhere],
        out_specs=local,
        scratch_shapes=[
            pltpu.VMEM((CH, TOK), bf16),
            pltpu.VMEM((CH, TOK), bf16),
            pltpu.VMEM((CH, TOK), bf16),
            pltpu.VMEM((CH // LANES, TOK // SUB * PITCH, LANES), f32),
            pltpu.VMEM((NC, MODES, 8, CH), f32),
            pltpu.VMEM((NC, MODES, CH), f32),
            pltpu.VMEM((MODES, 8, CH), f32),
            pltpu.VMEM((MODES, 8, CH), f32),
            pltpu.VMEM((MODES, 8, CH), f32),
            pltpu.VMEM((MODES, 8, CH), f32),
            pltpu.VMEM((3, MODES, CH), f32),
            pltpu.VMEM((MODES, CH), f32),
            pltpu.VMEM((CTX, MODES, CH), f32),
            pltpu.VMEM((NC, SLOTS * CH, CHUNK), bf16),
            pltpu.VMEM((SLOTS, 2, CH, CH), bf16),
            pltpu.VMEM((NC, CH, CHUNK), f32),
            pltpu.VMEM((NC, CH, CHUNK), bf16),
            pltpu.VMEM((NC, CH, CHUNK), bf16),
            pltpu.SemaphoreType.DMA((7,)),
            pltpu.SemaphoreType.DMA((10, NU)),
            pltpu.SemaphoreType.DMA((10, NU)),
            pltpu.SemaphoreType.DMA((CTX,)),
            pltpu.SemaphoreType.DMA((CTX,)),
            pltpu.SemaphoreType.DMA((SLOTS, 2, 2)),
            pltpu.SemaphoreType.DMA((SLOTS, 2, 2)),
            pltpu.SemaphoreType.DMA((5,)),
            pltpu.SemaphoreType.DMA((5,)),
            pltpu.SemaphoreType.REGULAR((4,)),
        ],
        compiler_params=pltpu.CompilerParams(
            collective_id=0, has_side_effects=True, vmem_limit_bytes=56 * 2**20
        ),
        name="hyena",
    )(
        key_feature, value_feature, query_gate, decay_rates, residues,
        skip_gain.reshape(1, CH), out_weight,
    )


def solution(mesh):
    return jax.shard_map(
        on_device,
        mesh=mesh,
        in_specs=(
            P("tp", "ctx"), P("tp", "ctx"), P("tp", "ctx"),
            P(None, "tp"), P(None, "tp"), P("tp"), P("tp", None),
        ),
        out_specs=P("tp", "ctx"),
        check_vma=False,
    )
```
